128 devices in a mesh: dp: 16 (over z, y_lo, core), head: 8 (over x, y_hi).
Axes of the slice: x: 4, y: 4 (y_hi: 2, y_lo: 2; y = y_hi * 2 + y_lo), z: 4, core: 2. Of those that a mesh axis runs over, the one named last changes fastest.
Arguments:
- resp_query: bfloat16 [16384, 8192], P(('dp', 'head')), may hold values from -6 to 6
- resp_keyval: bfloat16 [16384, 2048], P(('dp', 'head')), may hold values from -6 to 6
- grad_out: bfloat16 [16384, 8192], P(('dp', 'head')), may hold values from -6 to 6
- prompt_keyval: bfloat16 [8192, 2048], P('dp', 'head'), may hold values from -6 to 6
- response_prompt: int32 [32], P('dp'), may hold values from 0 to 7, as said below
- piece_owner: int32 [16], replicated, may hold values from 0 to 15, each once
Outputs:
- attn_out: bfloat16 [16384, 8192], P(('dp', 'head'))
- grad_query: bfloat16 [16384, 8192], P(('dp', 'head'))
- grad_keyval: bfloat16 [16384, 2048], P(('dp', 'head'))
- grad_prompt: bfloat16 [8192, 2048], P('dp', 'head')
The draws below stay inside these ranges and needn't reach their ends.
Inputs may be any that keep to these rules, and one draw needn't show every extreme that they name: `response_prompt`: every prompt has 2 to 8 responses; one prompt has exactly 8 and one exactly 2. `piece_owner`: each slot holds exactly one half of one prompt.
All inputs are finite; a program needn't handle non-finite values.
Results may differ from the reference program's by a relative error of at most 0.023.
Values may be sent and summed in bfloat16 or wider, within the bound.
A program may use at most 192 MiB of HBM per device.

```python
import jax
import jax.numpy as jnp
from jax import lax

QH = 64
KVH = 8
DH = 128
RL = 512
PLH = 512
RESP_DEV = 2
PL = 1024
PROMPTS = 8
RESPONSES = 32
RTOK = 16384
PROMPT_ROWS = 8192
N_DP = 16


def draw_resp_query(key, part):
    key = jax.random.fold_in(key, 11)
    groups = QH // KVH
    shape = (RESPONSES, RL, KVH, groups, DH)
    base = jnp.clip(jax.random.normal(key, shape), -6.0, 6.0)
    return base.reshape(RESPONSES * RL, QH * DH).astype(jnp.bfloat16)


def draw_prompt_keyval(key, part):
    key = jax.random.fold_in(key, 23)
    shape = (N_DP, PLH, KVH, 2, DH)
    base = jnp.clip(jax.random.normal(key, shape), -6.0, 6.0)
    return base.reshape(N_DP * PLH, KVH * 2 * DH).astype(jnp.bfloat16)


def draw_response_prompt(key, part):
    key = jax.random.fold_in(key, 5)
    first_key, second_key, third_key = jax.random.split(key, 3)
    ordering = jax.random.permutation(first_key, PROMPTS)
    counts = jnp.full((PROMPTS,), 2, jnp.int32).at[ordering[0]].set(8)
    movable = jnp.ones((PROMPTS,), bool).at[ordering[0]].set(False).at[ordering[1]].set(False)
    leftover = RESPONSES - 8 - 2 * (PROMPTS - 1)

    def add_one(step, counts):
        ranking = jax.random.randint(jax.random.fold_in(second_key, step), (PROMPTS,), 0, 1 << 20) * PROMPTS + jnp.arange(PROMPTS)
        ranking = jnp.where(movable & (counts < 8), ranking, -1)
        return counts.at[jnp.argmax(ranking)].add(1)
    counts = lax.fori_loop(0, leftover, add_one, counts)
    endings = jnp.cumsum(counts)
    places = jnp.arange(RESPONSES)
    labels = jnp.sum((places[:, None] >= endings[None, :]).astype(jnp.int32), axis=1)
    return jax.random.permutation(third_key, labels).astype(jnp.int32)


def block_levels(stream_key, shape, shards, low, largest):
    def one(position, blocks):
        heights = jax.random.uniform(jax.random.fold_in(jax.random.fold_in(stream_key, 6), position), (blocks,), jnp.float32, low / len(shards), largest / len(shards))
        return jnp.repeat(jnp.exp(heights), shape[position] // blocks).reshape((-1,) + (1,) * (len(shape) - position - 1))

    factor_of = one(*shards[0])
    for cut in shards[1:]:
        factor_of = factor_of * one(*cut)
    return factor_of


def centred(own_key, dims, spread, reach, cuts=(), dtype=jnp.bfloat16):
    values = jax.random.normal(own_key, dims, jnp.float32) * spread
    if len(cuts) > 0:
        values = block_levels(own_key, dims, cuts, -0.22, 0.18) * values
    return jnp.clip(values, min=-reach, max=reach).astype(dtype)


def setup_inputs(seed: int = 0) -> dict:
    key_of = jax.random.split(jax.random.key(seed), 7)
    return {
        "resp_query": draw_resp_query(jax.random.fold_in(key_of[6], 71), 0),
        "resp_keyval": centred(key_of[1], (RTOK, KVH * 2 * DH), 1.0, 6.0, ((0, 128),)),
        "grad_out": centred(key_of[2], (RTOK, QH * DH), 1.0, 6.0, ((0, 128),)),
        "prompt_keyval": draw_prompt_keyval(jax.random.fold_in(key_of[6], 71), 0),
        "response_prompt": draw_response_prompt(jax.random.fold_in(key_of[6], 71), 0),
        "piece_owner": jax.random.permutation(key_of[5], N_DP).astype(jnp.int32),
    }


NEGATIVE = -1.0e30


def to_bfloat(values):
    return lax.optimization_barrier(values.astype(jnp.bfloat16)).astype(jnp.float32)


def one_response(query, pair, cotangent, prompt_rows):
    score_scale = DH ** -0.5
    key_rows = jnp.concatenate([prompt_rows[:, :, 0], pair[:, :, 0]], axis=0).astype(jnp.float32)
    value_rows = jnp.concatenate([prompt_rows[:, :, 1], pair[:, :, 1]], axis=0).astype(jnp.float32)
    causal = jnp.arange(RL)[:, None] >= jnp.arange(RL)[None, :]
    allowed = jnp.concatenate([jnp.ones((RL, PL), bool), causal], axis=1)
    visible = allowed.astype(jnp.float32)
    query32 = query.astype(jnp.float32)
    cot32 = cotangent.astype(jnp.float32)
    scores = jnp.einsum("tkgd,skd->kgts", query32, key_rows) * score_scale
    masked = jnp.where(allowed, scores, NEGATIVE)
    maximum = jnp.max(masked, axis=-1)
    weights = jnp.exp(masked - maximum[..., None]) * visible
    normalizer = jnp.sum(weights, axis=-1)
    accumulated = jnp.einsum("kgts,skd->kgtd", to_bfloat(weights), value_rows)
    output = (accumulated / normalizer[..., None]).astype(jnp.bfloat16)
    log_total = maximum + jnp.log(normalizer)
    delta = jnp.einsum("tkgd,kgtd->kgt", cot32, output.astype(jnp.float32))
    probs = jnp.exp(masked - log_total[..., None]) * visible
    dprobs = jnp.einsum("tkgd,skd->kgts", cot32, value_rows)
    dscores = to_bfloat(probs * (dprobs - delta[..., None]) * score_scale)
    grad_q = jnp.einsum("kgts,skd->tkgd", dscores, key_rows)
    grad_k = jnp.einsum("kgts,tkgd->skd", dscores, query32)
    grad_v = jnp.einsum("kgts,tkgd->skd", to_bfloat(probs), cot32)
    return output.transpose(2, 0, 1, 3), grad_q.astype(jnp.bfloat16), jnp.stack([grad_k, grad_v], axis=2)


def reference(resp_query, resp_keyval, grad_out, prompt_keyval, response_prompt, piece_owner):
    groups = QH // KVH
    queries = resp_query.reshape(N_DP, RESP_DEV, RL, KVH, groups, DH)
    pairs = resp_keyval.reshape(N_DP, RESP_DEV, RL, KVH, 2, DH)
    cotangents = grad_out.reshape(N_DP, RESP_DEV, RL, KVH, groups, DH)
    stored = prompt_keyval.reshape(N_DP, PLH, KVH, 2, DH)
    assigned = response_prompt.reshape(N_DP, RESP_DEV).astype(jnp.int32)

    def device_step(summed, inputs):
        query, pair, cotangent, prompts = inputs
        partial_value = jnp.zeros((N_DP, PLH, KVH, 2, DH), jnp.float32)
        outputs, query_grads, pair_grads = [], [], []
        for response in range(RESP_DEV):
            first_slot = piece_owner[2 * prompts[response]].astype(jnp.int32)
            second_slot = piece_owner[2 * prompts[response] + 1].astype(jnp.int32)
            prompt_rows = jnp.concatenate([stored[first_slot], stored[second_slot]], axis=0)
            output, grad_q, both = one_response(query[response], pair[response], cotangent[response], prompt_rows)
            partial_value = partial_value.at[first_slot].add(both[:PLH])
            partial_value = partial_value.at[second_slot].add(both[PLH:PL])
            outputs.append(output)
            query_grads.append(grad_q)
            pair_grads.append(both[PL:].astype(jnp.bfloat16))
        summed = summed + to_bfloat(partial_value)
        return summed, (jnp.stack(outputs), jnp.stack(query_grads), jnp.stack(pair_grads))

    start = jnp.zeros((N_DP, PLH, KVH, 2, DH), jnp.float32)
    summed, (outputs, query_grads, pair_grads) = lax.scan(device_step, start, (queries, pairs, cotangents, assigned))
    attn_out = outputs.reshape(RTOK, QH * DH)
    grad_query = query_grads.reshape(RTOK, QH * DH)
    grad_keyval = pair_grads.reshape(RTOK, KVH * 2 * DH)
    grad_prompt = summed.astype(jnp.bfloat16).reshape(PROMPT_ROWS, KVH * 2 * DH)
    return (attn_out, grad_query, grad_keyval, grad_prompt)
```

```python
import functools
import math

import jax
import jax.numpy as jnp
from jax import lax
from jax.experimental import pallas as pl
from jax.experimental.pallas import tpu as pltpu
from jax.sharding import PartitionSpec as P

DH = 128
GROUPS = 8
BLK = 128
PLH = 512
PL = 2 * PLH
KEYS = PL + 4 * BLK
WIDE = 2 * DH
SPAN = GROUPS * DH

CH = 4
GH = GROUPS // CH
CW = GH * DH
NB = 2
ROWS = GH * NB * BLK
KC = 256

SCALE = DH ** (-0.5)
SCALE2 = SCALE * math.log2(math.e)
NEGATIVE = -1e30
MESH = pl.DeviceIdType.MESH
BF = jnp.bfloat16
F32 = jnp.float32


def dot(a, b, ca, cb):
    return lax.dot_general(a, b, (((ca,), (cb,)), ((), ())), preferred_element_type=F32)


def attend(first, q, do, k, v, kt, vt, s, e, d, dk, dv):
    edge = PL + BLK * first
    total = edge + BLK * NB
    spans = [(at, min(KC, total - at)) for at in range(0, total, KC)]
    top = None
    for at, n in spans:
        part = dot(k[at : at + n], q, 1, 1)
        if at + n > edge:
            key = lax.broadcasted_iota(jnp.int32, (n, BLK), 0) + (at - edge)
            tok = lax.broadcasted_iota(jnp.int32, (n, BLK), 1)
            seen = jnp.concatenate(
                [key <= tok + BLK * b for b in range(NB) for _ in range(GH)], axis=1
            )
            part = jnp.where(seen, part, NEGATIVE)
        s[at : at + n] = part
        high = jnp.max(part.reshape(n // 8, 8, ROWS), axis=0)
        top = high if top is None else jnp.maximum(top, high)
    peak = jnp.max(top, axis=0, keepdims=True) * SCALE2
    for at, n in spans:
        e[at : at + n] = jnp.exp2(s[at : at + n] * SCALE2 - peak).astype(BF)
    mixed = dot(vt[:, :total], e[:total], 1, 0)
    inverse = 1.0 / mixed[DH : DH + 1]
    out = (mixed[:DH] * inverse).astype(BF)
    cot = do.T.astype(F32)
    delta = jnp.sum(cot * out.astype(F32), axis=0, keepdims=True) * inverse
    scaled = (cot * inverse).astype(BF)
    for at, n in spans:
        dp = dot(v[at : at + n], scaled, 1, 0)
        d[at : at + n] = (e[at : at + n].astype(F32) * (dp - delta)).astype(BF)
    dq = (dot(kt[:, :total], d[:total], 1, 0) * SCALE).astype(BF)
    for at, n in spans:
        dk[at : at + n] += dot(d[at : at + n], q, 1, 0)
        dv[at : at + n] += dot(e[at : at + n], scaled, 1, 1)
    return out.T, dq.T


def kernel(
    q_hbm, do_hbm, kv_hbm, pk_hbm, rp, po,
    o_hbm, dq_hbm, dkv_hbm, gp_hbm,
    qbuf, dobuf, kvbuf, pbuf, kbuf, vbuf, ktbuf, vtbuf, sbuf, ebuf, dbuf, dkbuf, dvbuf,
    obuf, dqbuf, dkvbuf, asend, arecv, bsend, brecv, csend, crecv, gpbuf,
    q_s, q_r, do_s, do_r, kv_s, kv_r, p_s, p_r, o_s, o_r, dq_s, dq_r, dkv_s, dkv_r,
    a_s, a_r, b_s, b_r, c_s, c_r, g_s,
):
    dp = lax.axis_index("dp")
    me = lax.axis_index("head")
    x, yh = me // 2, lax.rem(me, 2)
    z, yl, core = dp // 4, lax.rem(dp // 2, 2), lax.rem(dp, 2)

    def slot_of(zz, yy, cc):
        return (lax.rem(zz + 4, 4) * 2 + yy) * 2 + cc

    other_core = (slot_of(z, yl, 1 - core), me)
    other_y = (slot_of(z, 1 - yl, core), me)
    up = (slot_of(z + 1, yl, core), me)
    down = (slot_of(z - 1, yl, core), me)
    far = (slot_of(z + 2, yl, core), me)
    steps = [(1, 1), (3, 1), (2, 0), (2, 1), (0, 1), (1, 0), (3, 0)]
    peers = [lax.rem(x + a, 4) * 2 + lax.rem(yh + b, 2) for a, b in steps]

    barrier = pltpu.get_barrier_semaphore()
    friends = [(dp, h) for h in peers] + [other_core, other_y, up, down, far]
    for friend in friends:
        pl.semaphore_signal(barrier, inc=1, device_id=friend, device_id_type=MESH)
    pl.semaphore_wait(barrier, len(friends))

    def send(src, dst, ssem, rsem, to):
        pltpu.make_async_remote_copy(
            src_ref=src, dst_ref=dst, send_sem=ssem, recv_sem=rsem, device_id=to, device_id_type=MESH
        ).start()

    def local(src, dst, sem):
        pltpu.make_async_copy(src, dst, sem).start()

    def drain(ref, sem):
        pltpu.make_async_copy(ref, ref, sem).wait()

    mine = slot_of(z, yl, core)
    for to in (other_y, up, down, other_core):
        send(pk_hbm, pbuf.at[mine], p_s, p_r.at[mine], to)
    local(pk_hbm, pbuf.at[mine], p_r.at[mine])

    def cols(h, width, offset=0):
        return pl.ds(pl.multiple_of(h * (width) + offset, DH), width)

    for h in peers:
        send(kv_hbm.at[:, cols(h, WIDE)], kvbuf.at[me], kv_s, kv_r, (dp, h))
    local(kv_hbm.at[:, cols(me, WIDE)], kvbuf.at[me], kv_r)

    def heads_of(h, c):
        return pl.ds(pl.multiple_of(h * SPAN + c * CW, DH), CW)

    def push(c, carry):
        for h in peers:
            send(q_hbm.at[:, heads_of(h, c)], qbuf.at[c, me], q_s, q_r.at[c], (dp, h))
            send(do_hbm.at[:, heads_of(h, c)], dobuf.at[c, me], do_s, do_r.at[c], (dp, h))
        local(q_hbm.at[:, heads_of(me, c)], qbuf.at[c, me], q_r.at[c])
        local(do_hbm.at[:, heads_of(me, c)], dobuf.at[c, me], do_r.at[c])
        return carry

    lax.fori_loop(0, CH, push, 0)

    def forward(slot, targets):
        drain(pbuf.at[slot], p_r.at[slot])
        for to in targets:
            send(pbuf.at[slot], pbuf.at[slot], p_s, p_r.at[slot], to)

    forward(slot_of(z, 1 - yl, core), (up, down, other_core))
    forward(slot_of(z + 1, 0, core), (down, other_core))
    forward(slot_of(z - 1, 1, core), (up, other_core))
    forward(slot_of(z + 1, 1, core), (other_core,))
    forward(slot_of(z - 1, 0, core), (other_core,))
    forward(slot_of(z + 2, 0, core), (other_core,))
    forward(slot_of(z + 2, 1, core), (other_core,))
    drain(pbuf.at[mine], p_r.at[mine])
    for zz in range(4):
        for yy in range(2):
            slot = slot_of(zz, yy, 1 - core)
            drain(pbuf.at[slot], p_r.at[slot])
    drain(kvbuf, kv_r)

    need = [[po[2 * rp[r] + half] for half in range(2)] for r in range(2)]
    for r in range(2):
        for half in range(2):
            rows = slice(half * PLH, (half + 1) * PLH)
            both = pbuf[need[r][half]]
            kbuf[r, rows] = both[:, :DH]
            vbuf[r, rows] = both[:, DH:]
            ktbuf[r, :, rows] = both[:, :DH].T
            vtbuf[r, :DH, rows] = both[:, DH:].T
        for b in range(4):
            rows = slice(PL + b * BLK, PL + (b + 1) * BLK)
            both = kvbuf[r * 4 + b]
            kbuf[r, rows] = both[:, :DH]
            vbuf[r, rows] = both[:, DH:]
            ktbuf[r, :, rows] = both[:, :DH].T
            vtbuf[r, :DH, rows] = both[:, DH:].T
        vtbuf[r, DH:] = jnp.ones((16, KEYS), BF)
    dkbuf[...] = jnp.zeros_like(dkbuf)
    dvbuf[...] = jnp.zeros_like(dvbuf)

    def give(buf, hbm, ssem, rsem, c, h):
        @pl.when(h != me)
        def _():
            send(buf.at[c, h], hbm.at[:, heads_of(me, c)], ssem, rsem, (dp, h))

        @pl.when(h == me)
        def _():
            local(buf.at[c, h], hbm.at[:, heads_of(me, c)], rsem)

    def work(i, carry):
        c, r = i // 2, lax.rem(i, 2)

        @pl.when(r == 0)
        def _():
            drain(qbuf.at[c], q_r.at[c])
            drain(dobuf.at[c], do_r.at[c])

        for first in range(0, 4, NB):
            tiles = [(r * 4 + first + b, j) for b in range(NB) for j in range(GH)]
            q = jnp.concatenate([qbuf[c, h, :, j * DH : (j + 1) * DH] for h, j in tiles], axis=0)
            do = jnp.concatenate([dobuf[c, h, :, j * DH : (j + 1) * DH] for h, j in tiles], axis=0)
            w = first // NB % 2
            out, dq = attend(
                first, q, do, kbuf.at[r], vbuf.at[r], ktbuf.at[r], vtbuf.at[r],
                sbuf.at[w], ebuf.at[w], dbuf.at[w], dkbuf.at[r], dvbuf.at[r],
            )
            for i_, (h, j) in enumerate(tiles):
                obuf[c, h, :, j * DH : (j + 1) * DH] = out[i_ * BLK : (i_ + 1) * BLK]
                dqbuf[c, h, :, j * DH : (j + 1) * DH] = dq[i_ * BLK : (i_ + 1) * BLK]
            for b in range(NB):
                give(obuf, o_hbm, o_s, o_r, c, r * 4 + first + b)
                give(dqbuf, dq_hbm, dq_s, dq_r, c, r * 4 + first + b)
        return carry

    lax.fori_loop(0, CH * 2, work, 0)

    def partial(slot):
        total = None
        for r in range(2):
            for half in range(2):
                rows = slice(half * PLH, (half + 1) * PLH)
                pick = jnp.where(need[r][half] == slot, 1.0, 0.0).astype(F32)
                block = jnp.concatenate(
                    [dkbuf[r, rows] * (pick * SCALE), dvbuf[r, rows] * pick], axis=1
                )
                total = block if total is None else total + block
        return total

    def away(n, carry):
        slot = n * 2 + (1 - core)
        asend[n] = partial(slot).astype(BF)
        send(asend.at[n], arecv.at[n], a_s, a_r.at[n], other_core)
        return carry

    lax.fori_loop(0, 8, away, 0)

    for b in range(8):
        r, at = b // 4, PL + (b % 4) * BLK
        dkvbuf[b, :, :DH] = (dkbuf[r, at : at + BLK] * SCALE).astype(BF)
        dkvbuf[b, :, DH:] = dvbuf[r, at : at + BLK].astype(BF)

        @pl.when(b != me)
        def _():
            send(dkvbuf.at[b], dkv_hbm.at[:, cols(me, WIDE)], dkv_s, dkv_r, (dp, b))

        @pl.when(b == me)
        def _():
            local(dkvbuf.at[b], dkv_hbm.at[:, cols(me, WIDE)], dkv_r)

    for hop, to in ((2, far), (1, up), (3, down)):
        for yy in range(2):
            n = lax.rem(z + hop, 4) * 2 + yy
            drain(arecv.at[n], a_r.at[n])
            bsend[hop - 1, yy] = (partial(n * 2 + core) + arecv[n].astype(F32)).astype(BF)
            send(
                bsend.at[hop - 1, yy], brecv.at[hop - 1, yy], b_s,
                b_r.at[(hop - 1) * 2 + yy], to,
            )

    def gathered(yy):
        n = z * 2 + yy
        total = partial(n * 2 + core) + arecv[n].astype(F32)
        for hop in range(3):
            total += brecv[hop, yy].astype(F32)
        return total

    for yy in range(2):
        drain(arecv.at[z * 2 + yy], a_r.at[z * 2 + yy])
        for hop in range(3):
            drain(brecv.at[hop, yy], b_r.at[hop * 2 + yy])
    csend[...] = gathered(1 - yl).astype(BF)
    send(csend, crecv, c_s, c_r, other_y)
    summed = gathered(yl)
    drain(crecv, c_r)
    gpbuf[...] = (summed + crecv[...].astype(F32)).astype(BF)
    local(gpbuf, gp_hbm, g_s)

    drain(gp_hbm, g_s)
    drain(o_hbm, o_r)
    drain(dq_hbm, dq_r)
    drain(dkv_hbm, dkv_r)
    drain(q_hbm.at[:, : 7 * SPAN], q_s)
    drain(do_hbm.at[:, : 7 * SPAN], do_s)
    drain(kv_hbm.at[:, : 7 * WIDE], kv_s)
    drain(pbuf.at[0:15], p_s)
    drain(obuf.at[:, 0:7], o_s)
    drain(dqbuf.at[:, 0:7], dq_s)
    drain(dkvbuf.at[0:7], dkv_s)
    drain(asend, a_s)
    drain(bsend, b_s)
    drain(csend, c_s)


def body(resp_query, resp_keyval, grad_out, prompt_keyval, response_prompt, piece_owner):
    tok = resp_query.shape[0]
    hbm = pl.BlockSpec(memory_space=pl.ANY)
    smem = pl.BlockSpec(memory_space=pltpu.SMEM)
    dma = pltpu.SemaphoreType.DMA
    shapes = [
        pltpu.VMEM((CH, 8, BLK, CW), BF),
        pltpu.VMEM((CH, 8, BLK, CW), BF),
        pltpu.VMEM((8, BLK, WIDE), BF),
        pltpu.VMEM((16, PLH, WIDE), BF),
        pltpu.VMEM((2, KEYS, DH), BF),
        pltpu.VMEM((2, KEYS, DH), BF),
        pltpu.VMEM((2, DH, KEYS), BF),
        pltpu.VMEM((2, DH + 16, KEYS), BF),
        pltpu.VMEM((2, KEYS, ROWS), F32),
        pltpu.VMEM((2, KEYS, ROWS), BF),
        pltpu.VMEM((2, KEYS, ROWS), BF),
        pltpu.VMEM((2, KEYS, DH), F32),
        pltpu.VMEM((2, KEYS, DH), F32),
        pltpu.VMEM((CH, 8, BLK, CW), BF),
        pltpu.VMEM((CH, 8, BLK, CW), BF),
        pltpu.VMEM((8, BLK, WIDE), BF),
        pltpu.VMEM((8, PLH, WIDE), BF),
        pltpu.VMEM((8, PLH, WIDE), BF),
        pltpu.VMEM((3, 2, PLH, WIDE), BF),
        pltpu.VMEM((3, 2, PLH, WIDE), BF),
        pltpu.VMEM((PLH, WIDE), BF),
        pltpu.VMEM((PLH, WIDE), BF),
        pltpu.VMEM((PLH, WIDE), BF),
    ]
    sems = [
        dma, dma((CH,)), dma, dma((CH,)), dma, dma, dma, dma((16,)),
        dma, dma, dma, dma, dma, dma,
        dma, dma((8,)), dma, dma((6,)), dma, dma, dma,
    ]
    return pl.pallas_call(
        kernel,
        out_shape=[
            jax.ShapeDtypeStruct((tok, 8 * SPAN), BF),
            jax.ShapeDtypeStruct((tok, 8 * SPAN), BF),
            jax.ShapeDtypeStruct((tok, 8 * WIDE), BF),
            jax.ShapeDtypeStruct((PLH, WIDE), BF),
        ],
        in_specs=[hbm, hbm, hbm, hbm, smem, smem],
        out_specs=[hbm, hbm, hbm, hbm],
        scratch_shapes=shapes + sems,
        compiler_params=pltpu.CompilerParams(
            collective_id=0, has_side_effects=True, vmem_limit_bytes=60 * 2**20
        ),
        name="attention",
    )(resp_query, grad_out, resp_keyval, prompt_keyval, response_prompt, piece_owner)


def solution(mesh):
    rows = P(("dp", "head"), None)
    placed = (rows, rows, rows, P("dp", "head"), P("dp"), P())
    return jax.shard_map(
        body,
        mesh=mesh,
        in_specs=placed,
        out_specs=(rows, rows, rows, P("dp", "head")),
        check_vma=False,
    )
```

```python
import functools
import math

import jax
import jax.numpy as jnp
from jax import lax
from jax.experimental import pallas as pl
from jax.experimental.pallas import tpu as pltpu
from jax.sharding import PartitionSpec as P

DH = 128
GROUPS = 8
BLK = 128
PLH = 512
PL = 2 * PLH
KEYS = PL + 4 * BLK
WIDE = 2 * DH
SPAN = GROUPS * DH

CH = 4
HELD = 2
SPLIT = 4
PARTS = (4, 4, 1, 1)
GH = GROUPS // CH
CW = GH * DH
NB = 2
ROWS = GH * NB * BLK
KC = 256

SCALE = DH ** (-0.5)
SCALE2 = SCALE * math.log2(math.e)
NEGATIVE = -1e30
MESH = pl.DeviceIdType.MESH
BF = jnp.bfloat16
F32 = jnp.float32


def dot(a, b, ca, cb):
    return lax.dot_general(a, b, (((ca,), (cb,)), ((), ())), preferred_element_type=F32)


def attend(first, q, do, k, v, kt, vt, s, e, d, dk, dv):
    edge = PL + BLK * first
    total = edge + BLK * NB
    spans = [(at, min(KC, total - at)) for at in range(0, total, KC)]
    top = None
    for at, n in spans:
        part = dot(k[at : at + n], q, 1, 1)
        if at + n > edge:
            key = lax.broadcasted_iota(jnp.int32, (n, BLK), 0) + (at - edge)
            tok = lax.broadcasted_iota(jnp.int32, (n, BLK), 1)
            seen = jnp.concatenate(
                [key <= tok + BLK * b for b in range(NB) for _ in range(GH)], axis=1
            )
            part = jnp.where(seen, part, NEGATIVE)
        s[at : at + n] = part
        high = jnp.max(part.reshape(n // 8, 8, ROWS), axis=0)
        top = high if top is None else jnp.maximum(top, high)
    peak = jnp.max(top, axis=0, keepdims=True) * SCALE2
    for at, n in spans:
        e[at : at + n] = jnp.exp2(s[at : at + n] * SCALE2 - peak).astype(BF)
    mixed = dot(vt[:, :total], e[:total], 1, 0)
    inverse = 1.0 / mixed[DH : DH + 1]
    out = (mixed[:DH] * inverse).astype(BF)
    cot = do.T.astype(F32)
    delta = jnp.sum(cot * out.astype(F32), axis=0, keepdims=True) * inverse
    scaled = (cot * inverse).astype(BF)
    for at, n in spans:
        dp = dot(v[at : at + n], scaled, 1, 0)
        d[at : at + n] = (e[at : at + n].astype(F32) * (dp - delta)).astype(BF)
    dq = (dot(kt[:, :total], d[:total], 1, 0) * SCALE).astype(BF)
    for at, n in spans:
        dk[at : at + n] += dot(d[at : at + n], q, 1, 0)
        dv[at : at + n] += dot(e[at : at + n], scaled, 1, 1)
    return out.T, dq.T


def kernel(
    q_hbm, do_hbm, kv_hbm, pk_hbm, rp, po,
    o_hbm, dq_hbm, dkv_hbm, gp_hbm,
    qbuf, dobuf, kvbuf, pbuf, kbuf, vbuf, ktbuf, vtbuf, sbuf, ebuf, dbuf, dkbuf, dvbuf,
    obuf, dqbuf, dkvbuf, asend, arecv, bsend, brecv, csend, crecv, gpbuf,
    q_s, q_r, do_s, do_r, kv_s, kv_r, p_s, p_r, o_s, o_r, dq_s, dq_r, dkv_s, dkv_r,
    a_s, a_r, b_s, b_r, c_s, c_r, g_s,
):
    dp = lax.axis_index("dp")
    me = lax.axis_index("head")
    x, yh = me // 2, lax.rem(me, 2)
    z, yl, core = dp // 4, lax.rem(dp // 2, 2), lax.rem(dp, 2)

    def slot_of(zz, yy, cc):
        return (lax.rem(zz + 4, 4) * 2 + yy) * 2 + cc

    other_core = (slot_of(z, yl, 1 - core), me)
    other_y = (slot_of(z, 1 - yl, core), me)
    up = (slot_of(z + 1, yl, core), me)
    down = (slot_of(z - 1, yl, core), me)
    steps = [(1, 1), (3, 1), (2, 0), (2, 1), (0, 1), (1, 0), (3, 0)]
    peers = [lax.rem(x + a, 4) * 2 + lax.rem(yh + b, 2) for a, b in steps]

    barrier = pltpu.get_barrier_semaphore()
    friends = [(dp, h) for h in peers] + [other_core, other_y, up, down]
    for friend in friends:
        pl.semaphore_signal(barrier, inc=1, device_id=friend, device_id_type=MESH)
    pl.semaphore_wait(barrier, len(friends))

    def send(src, dst, ssem, rsem, to):
        pltpu.make_async_remote_copy(
            src_ref=src, dst_ref=dst, send_sem=ssem, recv_sem=rsem, device_id=to, device_id_type=MESH
        ).start()

    def local(src, dst, sem):
        pltpu.make_async_copy(src, dst, sem).start()

    def drain(ref, sem):
        pltpu.make_async_copy(ref, ref, sem).wait()

    def mix(*queues):
        for turn in range(max(len(queue) for queue in queues)):
            for queue in queues:
                if turn < len(queue):
                    queue[turn]()

    def pieces(src, dst, ssem, rsem, to):
        rows = src.shape[0] // SPLIT
        return [
            functools.partial(
                send, src.at[pl.ds(n * rows, rows)], dst.at[pl.ds(n * rows, rows)], ssem, rsem, to
            )
            for n in range(SPLIT)
        ]

    mine = slot_of(z, yl, core)
    own_half = [
        pieces(pk_hbm, pbuf.at[mine], p_s, p_r.at[mine], to) for to in (other_y, up, down)
    ]
    send(pk_hbm, pbuf.at[mine], p_s, p_r.at[mine], other_core)
    local(pk_hbm, pbuf.at[mine], p_r.at[mine])

    def cols(h, width, offset=0):
        return pl.ds(pl.multiple_of(h * (width) + offset, DH), width)

    mix(
        *own_half,
        [
            functools.partial(
                send, kv_hbm.at[:, cols(h, WIDE)], kvbuf.at[me], kv_s, kv_r, (dp, h)
            )
            for h in peers
        ],
    )
    local(kv_hbm.at[:, cols(me, WIDE)], kvbuf.at[me], kv_r)

    def heads_of(h, c):
        return pl.ds(pl.multiple_of(h * SPAN + c * CW, DH), CW)

    def push_one(src, buf, ssem, rsem, c):
        local(src.at[:, heads_of(me, c)], buf.at[c, me], rsem.at[c])
        return [
            functools.partial(
                send, src.at[:, heads_of(h, c)], buf.at[c, me], ssem, rsem.at[c], (dp, h)
            )
            for h in peers
        ]

    def push_q(c):
        return push_one(q_hbm, qbuf, q_s, q_r, c)

    def push_do(c):
        return push_one(do_hbm, dobuf, do_s, do_r, c)

    def push(c, carry):
        mix(push_q(c), push_do(c))
        return carry

    def arrived(slot):
        drain(pbuf.at[slot], p_r.at[slot])
        send(pbuf.at[slot], pbuf.at[slot], p_s, p_r.at[slot], other_core)

    def onward(slot, to):
        return pieces(pbuf.at[slot], pbuf.at[slot], p_s, p_r.at[slot], to)

    near = slot_of(z, 1 - yl, core)
    arrived(near)
    mix(push_q(0), onward(near, up), onward(near, down))
    arrived(slot_of(z + 1, 0, core))
    arrived(slot_of(z - 1, 1, core))
    mix(
        push_do(0),
        onward(slot_of(z + 1, 0, core), down),
        onward(slot_of(z - 1, 1, core), up),
    )
    arrived(slot_of(z + 1, 1, core))
    arrived(slot_of(z - 1, 0, core))
    mix(push_q(1))
    dkbuf[...] = jnp.zeros_like(dkbuf)
    dvbuf[...] = jnp.zeros_like(dvbuf)
    drain(kvbuf, kv_r)
    for r in range(2):
        for b in range(4):
            rows = slice(PL + b * BLK, PL + (b + 1) * BLK)
            both = kvbuf[r * 4 + b]
            kbuf[r, rows] = both[:, :DH]
            vbuf[r, rows] = both[:, DH:]
            ktbuf[r, :, rows] = both[:, :DH].T
            vtbuf[r, :DH, rows] = both[:, DH:].T
        vtbuf[r, DH:] = jnp.ones((16, KEYS), BF)
    arrived(slot_of(z + 2, 0, core))
    arrived(slot_of(z + 2, 1, core))
    mix(push_do(1))
    lax.fori_loop(2, CH, push, 0)
    drain(pbuf.at[mine], p_r.at[mine])
    for zz in range(4):
        for yy in range(2):
            slot = slot_of(zz, yy, 1 - core)
            drain(pbuf.at[slot], p_r.at[slot])

    need = [[po[2 * rp[r] + half] for half in range(2)] for r in range(2)]
    for r in range(2):
        for half in range(2):
            rows = slice(half * PLH, (half + 1) * PLH)
            both = pbuf[need[r][half]]
            kbuf[r, rows] = both[:, :DH]
            vbuf[r, rows] = both[:, DH:]
            ktbuf[r, :, rows] = both[:, :DH].T
            vtbuf[r, :DH, rows] = both[:, DH:].T

    def give(c):
        queues = []
        for buf, hbm, ssem, rsem in ((obuf, o_hbm, o_s, o_r), (dqbuf, dq_hbm, dq_s, dq_r)):
            local(buf.at[c, me], hbm.at[:, heads_of(me, c)], rsem)
            queues.append(
                [
                    functools.partial(
                        send, buf.at[c, h], hbm.at[:, heads_of(me, c)], ssem, rsem, (dp, h)
                    )
                    for h in peers
                ]
            )
        return queues

    def work(i, carry):
        c, r = i // 2, lax.rem(i, 2)

        @pl.when(r == 0)
        def _():
            drain(qbuf.at[c], q_r.at[c])
            drain(dobuf.at[c], do_r.at[c])

        for first in range(0, 4, NB):
            tiles = [(r * 4 + first + b, j) for b in range(NB) for j in range(GH)]
            q = jnp.concatenate([qbuf[c, h, :, j * DH : (j + 1) * DH] for h, j in tiles], axis=0)
            do = jnp.concatenate([dobuf[c, h, :, j * DH : (j + 1) * DH] for h, j in tiles], axis=0)
            w = first // NB % 2
            out, dq = attend(
                first, q, do, kbuf.at[r], vbuf.at[r], ktbuf.at[r], vtbuf.at[r],
                sbuf.at[w], ebuf.at[w], dbuf.at[w], dkbuf.at[r], dvbuf.at[r],
            )
            for i_, (h, j) in enumerate(tiles):
                obuf[c, h, :, j * DH : (j + 1) * DH] = out[i_ * BLK : (i_ + 1) * BLK]
                dqbuf[c, h, :, j * DH : (j + 1) * DH] = dq[i_ * BLK : (i_ + 1) * BLK]

        @pl.when((r == 1) & (c < CH - HELD))
        def _():
            mix(*give(c))

        return carry

    lax.fori_loop(0, CH * 2, work, 0)

    def partial(slot):
        total = None
        for r in range(2):
            for half in range(2):
                rows = slice(half * PLH, (half + 1) * PLH)
                pick = jnp.where(need[r][half] == slot, 1.0, 0.0).astype(F32)
                block = jnp.concatenate(
                    [dkbuf[r, rows] * (pick * SCALE), dvbuf[r, rows] * pick], axis=1
                )
                total = block if total is None else total + block
        return total

    def pair_of(hop, yy):
        return lax.rem(z + hop, 4) * 2 + yy

    order = [(2, 0), (2, 1), (1, 1), (3, 0), (1, 0), (3, 1), (0, 0), (0, 1)]
    for hop, yy in order:
        n = pair_of(hop, yy)
        asend[n] = partial(n * 2 + (1 - core)).astype(BF)
        send(asend.at[n], arecv.at[n], a_s, a_r.at[n], other_core)

    def own_pair(hop, yy):
        n = pair_of(hop, yy)
        total = partial(n * 2 + core)
        drain(arecv.at[n], a_r.at[n])
        return total + arecv[n].astype(F32)

    def along(i, value, to):
        bsend[i] = value.astype(BF)
        return pieces(bsend.at[i], brecv.at[i], b_s, b_r.at[i], to)

    first_up = along(0, own_pair(2, 0), up)
    first_down = along(1, own_pair(2, 1), down)
    mix(first_up, first_down)
    second_up = along(2, own_pair(1, 1), up)
    second_down = along(3, own_pair(3, 0), down)
    mix(second_up, second_down, *give(CH - 2))
    last = []
    for i, hop, yy, to in ((0, 1, 0, up), (1, 3, 1, down)):
        total = own_pair(hop, yy)
        drain(brecv.at[i], b_r.at[i])
        last.append(along(4 + i, total + brecv[i].astype(F32), to))

    for b in range(8):
        r, at = b // 4, PL + (b % 4) * BLK
        dkvbuf[b, :, :DH] = (dkbuf[r, at : at + BLK] * SCALE).astype(BF)
        dkvbuf[b, :, DH:] = dvbuf[r, at : at + BLK].astype(BF)
    pairs_out = [
        functools.partial(
            send, dkvbuf.at[h], dkv_hbm.at[:, cols(me, WIDE)], dkv_s, dkv_r, (dp, h)
        )
        for h in peers
    ]
    local(dkvbuf.at[me], dkv_hbm.at[:, cols(me, WIDE)], dkv_r)
    mix(*last, pairs_out, *give(CH - 1))

    zero_half = own_pair(0, 0)
    one_half = own_pair(0, 1)
    for i in (2, 3, 4, 5):
        drain(brecv.at[i], b_r.at[i])
    zero_half += brecv[3].astype(F32) + brecv[4].astype(F32)
    one_half += brecv[2].astype(F32) + brecv[5].astype(F32)
    low = yl == 0
    csend[...] = jnp.where(low, one_half, zero_half).astype(BF)
    mix(pieces(csend, crecv, c_s, c_r, other_y))
    kept = jnp.where(low, zero_half, one_half)
    drain(crecv, c_r)
    gpbuf[...] = (kept + crecv[...].astype(F32)).astype(BF)
    local(gpbuf, gp_hbm, g_s)

    drain(gp_hbm, g_s)
    drain(o_hbm, o_r)
    drain(dq_hbm, dq_r)
    drain(dkv_hbm, dkv_r)
    drain(q_hbm.at[:, : 7 * SPAN], q_s)
    drain(do_hbm.at[:, : 7 * SPAN], do_s)
    drain(kv_hbm.at[:, : 7 * WIDE], kv_s)
    drain(pbuf.at[0:15], p_s)
    drain(obuf.at[:, 0:7], o_s)
    drain(dqbuf.at[:, 0:7], dq_s)
    drain(dkvbuf.at[0:7], dkv_s)
    drain(asend, a_s)
    drain(bsend, b_s)
    drain(csend, c_s)


def settle(*refs):
    sources, targets, stages = refs[:4], refs[4:8], refs[8:12]
    into, out = refs[12:]
    moves = []
    for src, dst, stage, parts in zip(sources, targets, stages, PARTS):
        rows = src.shape[0] // parts
        for n in range(parts):
            at, i = pl.ds(n * rows, rows), len(moves)
            moves.append(
                (
                    pltpu.make_async_copy(src.at[at], stage.at[at], into.at[i]),
                    pltpu.make_async_copy(stage.at[at], dst.at[at], out.at[i]),
                )
            )
    for first, _ in moves:
        first.start()
    for first, second in moves:
        first.wait()
        second.start()
    for _, second in moves:
        second.wait()


def body(resp_query, resp_keyval, grad_out, prompt_keyval, response_prompt, piece_owner):
    tok = resp_query.shape[0]
    hbm = pl.BlockSpec(memory_space=pl.ANY)
    smem = pl.BlockSpec(memory_space=pltpu.SMEM)
    dma = pltpu.SemaphoreType.DMA
    shapes = [
        pltpu.VMEM((CH, 8, BLK, CW), BF),
        pltpu.VMEM((CH, 8, BLK, CW), BF),
        pltpu.VMEM((8, BLK, WIDE), BF),
        pltpu.VMEM((16, PLH, WIDE), BF),
        pltpu.VMEM((2, KEYS, DH), BF),
        pltpu.VMEM((2, KEYS, DH), BF),
        pltpu.VMEM((2, DH, KEYS), BF),
        pltpu.VMEM((2, DH + 16, KEYS), BF),
        pltpu.VMEM((2, KEYS, ROWS), F32),
        pltpu.VMEM((2, KEYS, ROWS), BF),
        pltpu.VMEM((2, KEYS, ROWS), BF),
        pltpu.VMEM((2, KEYS, DH), F32),
        pltpu.VMEM((2, KEYS, DH), F32),
        pltpu.VMEM((CH, 8, BLK, CW), BF),
        pltpu.VMEM((CH, 8, BLK, CW), BF),
        pltpu.VMEM((8, BLK, WIDE), BF),
        pltpu.VMEM((8, PLH, WIDE), BF),
        pltpu.VMEM((8, PLH, WIDE), BF),
        pltpu.VMEM((6, PLH, WIDE), BF),
        pltpu.VMEM((6, PLH, WIDE), BF),
        pltpu.VMEM((PLH, WIDE), BF),
        pltpu.VMEM((PLH, WIDE), BF),
        pltpu.VMEM((PLH, WIDE), BF),
    ]
    sems = [
        dma, dma((CH,)), dma, dma((CH,)), dma, dma, dma, dma((16,)),
        dma, dma, dma, dma, dma, dma,
        dma, dma((8,)), dma, dma((6,)), dma, dma, dma,
    ]
    made = pl.pallas_call(
        kernel,
        out_shape=[
            jax.ShapeDtypeStruct((tok, 8 * SPAN), BF),
            jax.ShapeDtypeStruct((tok, 8 * SPAN), BF),
            jax.ShapeDtypeStruct((tok, 8 * WIDE), BF),
            jax.ShapeDtypeStruct((PLH, WIDE), BF),
        ],
        in_specs=[hbm, hbm, hbm, hbm, smem, smem],
        out_specs=[hbm, hbm, hbm, hbm],
        scratch_shapes=shapes + sems,
        compiler_params=pltpu.CompilerParams(
            collective_id=0, has_side_effects=True, vmem_limit_bytes=60 * 2**20
        ),
        name="attention",
    )(resp_query, grad_out, resp_keyval, prompt_keyval, response_prompt, piece_owner)
    return pl.pallas_call(
        settle,
        out_shape=[jax.ShapeDtypeStruct(a.shape, a.dtype) for a in made],
        in_specs=[hbm] * 4,
        out_specs=[hbm] * 4,
        scratch_shapes=[pltpu.VMEM(a.shape, a.dtype) for a in made] + [dma((sum(PARTS),))] * 2,
        compiler_params=pltpu.CompilerParams(vmem_limit_bytes=60 * 2**20),
        name="settle",
    )(*made)


def solution(mesh):
    rows = P(("dp", "head"), None)
    placed = (rows, rows, rows, P("dp", "head"), P("dp"), P())
    return jax.shard_map(
        body,
        mesh=mesh,
        in_specs=placed,
        out_specs=(rows, rows, rows, P("dp", "head")),
        check_vma=False,
    )
```

```python
import functools
import math

import jax
import jax.numpy as jnp
from jax import lax
from jax.experimental import pallas as pl
from jax.experimental.pallas import tpu as pltpu
from jax.sharding import PartitionSpec as P

DH = 128
GROUPS = 8
BLK = 128
PLH = 512
PL = 2 * PLH
KEYS = PL + 4 * BLK
WIDE = 2 * DH
SPAN = GROUPS * DH

CH = 4
HELD = 2
SPLIT = 2
PARTS = (1, 1, 1, 1)
GH = GROUPS // CH
CW = GH * DH
NB = 2
ROWS = GH * NB * BLK
KC = 256

SCALE = DH ** (-0.5)
SCALE2 = SCALE * math.log2(math.e)
NEGATIVE = -1e30
MESH = pl.DeviceIdType.MESH
BF = jnp.bfloat16
F32 = jnp.float32


def dot(a, b, ca, cb):
    return lax.dot_general(a, b, (((ca,), (cb,)), ((), ())), preferred_element_type=F32)


def attend(first, q, do, k, v, kt, vt, s, e, d, dk, dv):
    edge = PL + BLK * first
    total = edge + BLK * NB
    spans = [(at, min(KC, total - at)) for at in range(0, total, KC)]
    top = None
    for at, n in spans:
        part = dot(k[at : at + n], q, 1, 1)
        if at + n > edge:
            key = lax.broadcasted_iota(jnp.int32, (n, BLK), 0) + (at - edge)
            tok = lax.broadcasted_iota(jnp.int32, (n, BLK), 1)
            seen = jnp.concatenate(
                [key <= tok + BLK * b for b in range(NB) for _ in range(GH)], axis=1
            )
            part = jnp.where(seen, part, NEGATIVE)
        s[at : at + n] = part
        high = jnp.max(part.reshape(n // 8, 8, ROWS), axis=0)
        top = high if top is None else jnp.maximum(top, high)
    peak = jnp.max(top, axis=0, keepdims=True) * SCALE2
    for at, n in spans:
        e[at : at + n] = jnp.exp2(s[at : at + n] * SCALE2 - peak).astype(BF)
    mixed = dot(vt[:, :total], e[:total], 1, 0)
    inverse = 1.0 / mixed[DH : DH + 1]
    out = (mixed[:DH] * inverse).astype(BF)
    cot = do.T.astype(F32)
    delta = jnp.sum(cot * out.astype(F32), axis=0, keepdims=True) * inverse
    scaled = (cot * inverse).astype(BF)
    for at, n in spans:
        dp = dot(v[at : at + n], scaled, 1, 0)
        d[at : at + n] = (e[at : at + n].astype(F32) * (dp - delta)).astype(BF)
    dq = (dot(kt[:, :total], d[:total], 1, 0) * SCALE).astype(BF)
    for at, n in spans:
        dk[at : at + n] += dot(d[at : at + n], q, 1, 0)
        dv[at : at + n] += dot(e[at : at + n], scaled, 1, 1)
    return out.T, dq.T


def kernel(
    q_hbm, do_hbm, kv_hbm, pk_hbm, rp, po,
    o_hbm, dq_hbm, dkv_hbm, gp_hbm,
    qbuf, dobuf, kvbuf, pbuf, kbuf, vbuf, ktbuf, vtbuf, sbuf, ebuf, dbuf, dkbuf, dvbuf,
    obuf, dqbuf, dkvbuf, asend, arecv, bsend, brecv, csend, crecv, gpbuf,
    q_s, q_r, do_s, do_r, kv_s, kv_r, p_s, p_r, o_s, o_r, dq_s, dq_r, dkv_s, dkv_r,
    a_s, a_r, b_s, b_r, c_s, c_r, g_s,
):
    dp = lax.axis_index("dp")
    me = lax.axis_index("head")
    x, yh = me // 2, lax.rem(me, 2)
    z, yl, core = dp // 4, lax.rem(dp // 2, 2), lax.rem(dp, 2)

    def slot_of(zz, yy, cc):
        return (lax.rem(zz + 4, 4) * 2 + yy) * 2 + cc

    other_core = (slot_of(z, yl, 1 - core), me)
    other_y = (slot_of(z, 1 - yl, core), me)
    up = (slot_of(z + 1, yl, core), me)
    down = (slot_of(z - 1, yl, core), me)
    steps = [(2, 1), (1, 0), (3, 1), (2, 0), (1, 1), (3, 0), (0, 1)]
    peers = [lax.rem(x + a, 4) * 2 + lax.rem(yh + b, 2) for a, b in steps]

    barrier = pltpu.get_barrier_semaphore()
    friends = [(dp, h) for h in peers] + [other_core, other_y, up, down]
    for friend in friends:
        pl.semaphore_signal(barrier, inc=1, device_id=friend, device_id_type=MESH)
    pl.semaphore_wait(barrier, len(friends))

    def send(src, dst, ssem, rsem, to):
        pltpu.make_async_remote_copy(
            src_ref=src, dst_ref=dst, send_sem=ssem, recv_sem=rsem, device_id=to, device_id_type=MESH
        ).start()

    def local(src, dst, sem):
        pltpu.make_async_copy(src, dst, sem).start()

    def drain(ref, sem):
        pltpu.make_async_copy(ref, ref, sem).wait()

    def mix(*queues):
        for turn in range(max(len(queue) for queue in queues)):
            for queue in queues:
                if turn < len(queue):
                    queue[turn]()

    def pieces(src, dst, ssem, rsem, to):
        rows = src.shape[0] // SPLIT
        return [
            functools.partial(
                send, src.at[pl.ds(n * rows, rows)], dst.at[pl.ds(n * rows, rows)], ssem, rsem, to
            )
            for n in range(SPLIT)
        ]

    mine = slot_of(z, yl, core)
    own_half = [
        pieces(pk_hbm, pbuf.at[mine], p_s, p_r.at[mine], to) for to in (other_y, up, down)
    ]
    send(pk_hbm, pbuf.at[mine], p_s, p_r.at[mine], other_core)
    local(pk_hbm, pbuf.at[mine], p_r.at[mine])

    def cols(h, width, offset=0):
        return pl.ds(pl.multiple_of(h * (width) + offset, DH), width)

    mix(
        *own_half,
        [
            functools.partial(
                send, kv_hbm.at[:, cols(h, WIDE)], kvbuf.at[me], kv_s, kv_r, (dp, h)
            )
            for h in peers
        ],
    )
    local(kv_hbm.at[:, cols(me, WIDE)], kvbuf.at[me], kv_r)

    def heads_of(h, c):
        return pl.ds(pl.multiple_of(h * SPAN + c * CW, DH), CW)

    def push_one(src, buf, ssem, rsem, c):
        local(src.at[:, heads_of(me, c)], buf.at[c, me], rsem.at[c])
        return [
            functools.partial(
                send, src.at[:, heads_of(h, c)], buf.at[c, me], ssem, rsem.at[c], (dp, h)
            )
            for h in peers
        ]

    def push_q(c):
        return push_one(q_hbm, qbuf, q_s, q_r, c)

    def push_do(c):
        return push_one(do_hbm, dobuf, do_s, do_r, c)

    def push(c, carry):
        mix(push_q(c), push_do(c))
        return carry

    def arrived(slot):
        drain(pbuf.at[slot], p_r.at[slot])
        send(pbuf.at[slot], pbuf.at[slot], p_s, p_r.at[slot], other_core)

    def onward(slot, to):
        return pieces(pbuf.at[slot], pbuf.at[slot], p_s, p_r.at[slot], to)

    near = slot_of(z, 1 - yl, core)
    arrived(near)
    mix(onward(near, up), onward(near, down), push_q(0), push_do(0))
    arrived(slot_of(z + 1, 0, core))
    arrived(slot_of(z - 1, 1, core))
    mix(
        push_q(1),
        onward(slot_of(z + 1, 0, core), down),
        onward(slot_of(z - 1, 1, core), up),
    )
    arrived(slot_of(z + 1, 1, core))
    arrived(slot_of(z - 1, 0, core))
    mix(push_do(1))
    dkbuf[...] = jnp.zeros_like(dkbuf)
    dvbuf[...] = jnp.zeros_like(dvbuf)
    drain(kvbuf, kv_r)
    for r in range(2):
        for b in range(4):
            rows = slice(PL + b * BLK, PL + (b + 1) * BLK)
            both = kvbuf[r * 4 + b]
            kbuf[r, rows] = both[:, :DH]
            vbuf[r, rows] = both[:, DH:]
            ktbuf[r, :, rows] = both[:, :DH].T
            vtbuf[r, :DH, rows] = both[:, DH:].T
        vtbuf[r, DH:] = jnp.ones((16, KEYS), BF)
    arrived(slot_of(z + 2, 0, core))
    arrived(slot_of(z + 2, 1, core))
    lax.fori_loop(2, CH, push, 0)
    drain(pbuf.at[mine], p_r.at[mine])
    for zz in range(4):
        for yy in range(2):
            slot = slot_of(zz, yy, 1 - core)
            drain(pbuf.at[slot], p_r.at[slot])

    need = [[po[2 * rp[r] + half] for half in range(2)] for r in range(2)]
    for r in range(2):
        for half in range(2):
            rows = slice(half * PLH, (half + 1) * PLH)
            both = pbuf[need[r][half]]
            kbuf[r, rows] = both[:, :DH]
            vbuf[r, rows] = both[:, DH:]
            ktbuf[r, :, rows] = both[:, :DH].T
            vtbuf[r, :DH, rows] = both[:, DH:].T

    def give(c):
        queues = []
        for buf, hbm, ssem, rsem in ((obuf, o_hbm, o_s, o_r), (dqbuf, dq_hbm, dq_s, dq_r)):
            local(buf.at[c, me], hbm.at[:, heads_of(me, c)], rsem)
            queues.append(
                [
                    functools.partial(
                        send, buf.at[c, h], hbm.at[:, heads_of(me, c)], ssem, rsem, (dp, h)
                    )
                    for h in peers
                ]
            )
        return queues

    def work(i, carry):
        c, r = i // 2, lax.rem(i, 2)

        @pl.when(r == 0)
        def _():
            drain(qbuf.at[c], q_r.at[c])
            drain(dobuf.at[c], do_r.at[c])

        for first in range(0, 4, NB):
            tiles = [(r * 4 + first + b, j) for b in range(NB) for j in range(GH)]
            q = jnp.concatenate([qbuf[c, h, :, j * DH : (j + 1) * DH] for h, j in tiles], axis=0)
            do = jnp.concatenate([dobuf[c, h, :, j * DH : (j + 1) * DH] for h, j in tiles], axis=0)
            w = first // NB % 2
            out, dq = attend(
                first, q, do, kbuf.at[r], vbuf.at[r], ktbuf.at[r], vtbuf.at[r],
                sbuf.at[w], ebuf.at[w], dbuf.at[w], dkbuf.at[r], dvbuf.at[r],
            )
            for i_, (h, j) in enumerate(tiles):
                obuf[c, h, :, j * DH : (j + 1) * DH] = out[i_ * BLK : (i_ + 1) * BLK]
                dqbuf[c, h, :, j * DH : (j + 1) * DH] = dq[i_ * BLK : (i_ + 1) * BLK]

        @pl.when((r == 1) & (c < CH - HELD))
        def _():
            mix(*give(c))

        return carry

    lax.fori_loop(0, CH * 2, work, 0)

    def partial(slot):
        total = None
        for r in range(2):
            for half in range(2):
                rows = slice(half * PLH, (half + 1) * PLH)
                pick = jnp.where(need[r][half] == slot, 1.0, 0.0).astype(F32)
                block = jnp.concatenate(
                    [dkbuf[r, rows] * (pick * SCALE), dvbuf[r, rows] * pick], axis=1
                )
                total = block if total is None else total + block
        return total

    def pair_of(hop, yy):
        return lax.rem(z + hop, 4) * 2 + yy

    order = [(2, 0), (2, 1), (1, 1), (3, 0), (1, 0), (3, 1), (0, 0), (0, 1)]
    for hop, yy in order:
        n = pair_of(hop, yy)
        asend[n] = partial(n * 2 + (1 - core)).astype(BF)
        send(asend.at[n], arecv.at[n], a_s, a_r.at[n], other_core)

    def own_pair(hop, yy):
        n = pair_of(hop, yy)
        total = partial(n * 2 + core)
        drain(arecv.at[n], a_r.at[n])
        return total + arecv[n].astype(F32)

    def along(i, value, to):
        bsend[i] = value.astype(BF)
        return pieces(bsend.at[i], brecv.at[i], b_s, b_r.at[i], to)

    first_up = along(0, own_pair(2, 0), up)
    first_down = along(1, own_pair(2, 1), down)
    mix(first_up, first_down)
    second_up = along(2, own_pair(1, 1), up)
    second_down = along(3, own_pair(3, 0), down)
    mix(second_up, second_down, *give(CH - 2))
    last = []
    for i, hop, yy, to in ((0, 1, 0, up), (1, 3, 1, down)):
        total = own_pair(hop, yy)
        drain(brecv.at[i], b_r.at[i])
        last.append(along(4 + i, total + brecv[i].astype(F32), to))

    for b in range(8):
        r, at = b // 4, PL + (b % 4) * BLK
        dkvbuf[b, :, :DH] = (dkbuf[r, at : at + BLK] * SCALE).astype(BF)
        dkvbuf[b, :, DH:] = dvbuf[r, at : at + BLK].astype(BF)
    pairs_out = [
        functools.partial(
            send, dkvbuf.at[h], dkv_hbm.at[:, cols(me, WIDE)], dkv_s, dkv_r, (dp, h)
        )
        for h in peers
    ]
    local(dkvbuf.at[me], dkv_hbm.at[:, cols(me, WIDE)], dkv_r)
    mix(*last, pairs_out, *give(CH - 1))

    zero_half = own_pair(0, 0)
    one_half = own_pair(0, 1)
    for i in (2, 3, 4, 5):
        drain(brecv.at[i], b_r.at[i])
    zero_half += brecv[3].astype(F32) + brecv[4].astype(F32)
    one_half += brecv[2].astype(F32) + brecv[5].astype(F32)
    low = yl == 0
    csend[...] = jnp.where(low, one_half, zero_half).astype(BF)
    mix(pieces(csend, crecv, c_s, c_r, other_y))
    kept = jnp.where(low, zero_half, one_half)
    drain(crecv, c_r)
    gpbuf[...] = (kept + crecv[...].astype(F32)).astype(BF)
    local(gpbuf, gp_hbm, g_s)

    drain(gp_hbm, g_s)
    drain(o_hbm, o_r)
    drain(dq_hbm, dq_r)
    drain(dkv_hbm, dkv_r)
    drain(q_hbm.at[:, : 7 * SPAN], q_s)
    drain(do_hbm.at[:, : 7 * SPAN], do_s)
    drain(kv_hbm.at[:, : 7 * WIDE], kv_s)
    drain(pbuf.at[0:15], p_s)
    drain(obuf.at[:, 0:7], o_s)
    drain(dqbuf.at[:, 0:7], dq_s)
    drain(dkvbuf.at[0:7], dkv_s)
    drain(asend, a_s)
    drain(bsend, b_s)
    drain(csend, c_s)


def settle(*refs):
    sources, targets, stages = refs[:4], refs[4:8], refs[8:12]
    into, out = refs[12:]
    moves = []
    for src, dst, stage, parts in zip(sources, targets, stages, PARTS):
        rows = src.shape[0] // parts
        for n in range(parts):
            at, i = pl.ds(n * rows, rows), len(moves)
            moves.append(
                (
                    pltpu.make_async_copy(src.at[at], stage.at[at], into.at[i]),
                    pltpu.make_async_copy(stage.at[at], dst.at[at], out.at[i]),
                )
            )
    for first, _ in moves:
        first.start()
    for first, second in moves:
        first.wait()
        second.start()
    for _, second in moves:
        second.wait()


def body(resp_query, resp_keyval, grad_out, prompt_keyval, response_prompt, piece_owner):
    tok = resp_query.shape[0]
    hbm = pl.BlockSpec(memory_space=pl.ANY)
    smem = pl.BlockSpec(memory_space=pltpu.SMEM)
    dma = pltpu.SemaphoreType.DMA
    shapes = [
        pltpu.VMEM((CH, 8, BLK, CW), BF),
        pltpu.VMEM((CH, 8, BLK, CW), BF),
        pltpu.VMEM((8, BLK, WIDE), BF),
        pltpu.VMEM((16, PLH, WIDE), BF),
        pltpu.VMEM((2, KEYS, DH), BF),
        pltpu.VMEM((2, KEYS, DH), BF),
        pltpu.VMEM((2, DH, KEYS), BF),
        pltpu.VMEM((2, DH + 16, KEYS), BF),
        pltpu.VMEM((2, KEYS, ROWS), F32),
        pltpu.VMEM((2, KEYS, ROWS), BF),
        pltpu.VMEM((2, KEYS, ROWS), BF),
        pltpu.VMEM((2, KEYS, DH), F32),
        pltpu.VMEM((2, KEYS, DH), F32),
        pltpu.VMEM((CH, 8, BLK, CW), BF),
        pltpu.VMEM((CH, 8, BLK, CW), BF),
        pltpu.VMEM((8, BLK, WIDE), BF),
        pltpu.VMEM((8, PLH, WIDE), BF),
        pltpu.VMEM((8, PLH, WIDE), BF),
        pltpu.VMEM((6, PLH, WIDE), BF),
        pltpu.VMEM((6, PLH, WIDE), BF),
        pltpu.VMEM((PLH, WIDE), BF),
        pltpu.VMEM((PLH, WIDE), BF),
        pltpu.VMEM((PLH, WIDE), BF),
    ]
    sems = [
        dma, dma((CH,)), dma, dma((CH,)), dma, dma, dma, dma((16,)),
        dma, dma, dma, dma, dma, dma,
        dma, dma((8,)), dma, dma((6,)), dma, dma, dma,
    ]
    made = pl.pallas_call(
        kernel,
        out_shape=[
            jax.ShapeDtypeStruct((tok, 8 * SPAN), BF),
            jax.ShapeDtypeStruct((tok, 8 * SPAN), BF),
            jax.ShapeDtypeStruct((tok, 8 * WIDE), BF),
            jax.ShapeDtypeStruct((PLH, WIDE), BF),
        ],
        in_specs=[hbm, hbm, hbm, hbm, smem, smem],
        out_specs=[hbm, hbm, hbm, hbm],
        scratch_shapes=shapes + sems,
        compiler_params=pltpu.CompilerParams(
            collective_id=0, has_side_effects=True, vmem_limit_bytes=60 * 2**20
        ),
        name="attention",
    )(resp_query, grad_out, resp_keyval, prompt_keyval, response_prompt, piece_owner)
    return pl.pallas_call(
        settle,
        out_shape=[jax.ShapeDtypeStruct(a.shape, a.dtype) for a in made],
        in_specs=[hbm] * 4,
        out_specs=[hbm] * 4,
        scratch_shapes=[pltpu.VMEM(a.shape, a.dtype) for a in made] + [dma((sum(PARTS),))] * 2,
        compiler_params=pltpu.CompilerParams(vmem_limit_bytes=60 * 2**20),
        name="settle",
    )(*made)


def solution(mesh):
    rows = P(("dp", "head"), None)
    placed = (rows, rows, rows, P("dp", "head"), P("dp"), P())
    return jax.shard_map(
        body,
        mesh=mesh,
        in_specs=placed,
        out_specs=(rows, rows, rows, P("dp", "head")),
        check_vma=False,
    )
```

```python
import functools
import math

import jax
import jax.numpy as jnp
from jax import lax
from jax.experimental import pallas as pl
from jax.experimental.pallas import tpu as pltpu
from jax.sharding import PartitionSpec as P

DH = 128
GROUPS = 8
BLK = 128
PLH = 512
PL = 2 * PLH
KEYS = PL + 4 * BLK
WIDE = 2 * DH
SPAN = GROUPS * DH

CH = 4
HELD = 1
SPLIT = 2
PARTS = (1, 1, 1, 1)
GH = GROUPS // CH
CW = GH * DH
NB = 2
ROWS = GH * NB * BLK
KC = 256

SCALE = DH ** (-0.5)
SCALE2 = SCALE * math.log2(math.e)
NEGATIVE = -1e30
MESH = pl.DeviceIdType.MESH
BF = jnp.bfloat16
F32 = jnp.float32


def dot(a, b, ca, cb):
    return lax.dot_general(a, b, (((ca,), (cb,)), ((), ())), preferred_element_type=F32)


def attend(first, q, do, k, v, kt, vt, s, e, d, dk, dv):
    edge = PL + BLK * first
    total = edge + BLK * NB
    spans = [(at, min(KC, total - at)) for at in range(0, total, KC)]
    top = None
    for at, n in spans:
        part = dot(k[at : at + n], q, 1, 1)
        if at + n > edge:
            key = lax.broadcasted_iota(jnp.int32, (n, BLK), 0) + (at - edge)
            tok = lax.broadcasted_iota(jnp.int32, (n, BLK), 1)
            seen = jnp.concatenate(
                [key <= tok + BLK * b for b in range(NB) for _ in range(GH)], axis=1
            )
            part = jnp.where(seen, part, NEGATIVE)
        s[at : at + n] = part
        high = jnp.max(part.reshape(n // 8, 8, ROWS), axis=0)
        top = high if top is None else jnp.maximum(top, high)
    peak = jnp.max(top, axis=0, keepdims=True) * SCALE2
    for at, n in spans:
        e[at : at + n] = jnp.exp2(s[at : at + n] * SCALE2 - peak).astype(BF)
    mixed = dot(vt[:, :total], e[:total], 1, 0)
    inverse = 1.0 / mixed[DH : DH + 1]
    out = (mixed[:DH] * inverse).astype(BF)
    cot = do.T.astype(F32)
    delta = jnp.sum(cot * out.astype(F32), axis=0, keepdims=True) * inverse
    scaled = (cot * inverse).astype(BF)
    for at, n in spans:
        dp = dot(v[at : at + n], scaled, 1, 0)
        d[at : at + n] = (e[at : at + n].astype(F32) * (dp - delta)).astype(BF)
    dq = (dot(kt[:, :total], d[:total], 1, 0) * SCALE).astype(BF)
    for at, n in spans:
        dk[at : at + n] += dot(d[at : at + n], q, 1, 0)
        dv[at : at + n] += dot(e[at : at + n], scaled, 1, 1)
    return out.T, dq.T


def kernel(
    q_hbm, do_hbm, kv_hbm, pk_hbm, rp, po,
    o_hbm, dq_hbm, dkv_hbm, gp_hbm,
    qbuf, dobuf, kvbuf, pbuf, kbuf, vbuf, ktbuf, vtbuf, sbuf, ebuf, dbuf, dkbuf, dvbuf,
    obuf, dqbuf, dkvbuf, asend, arecv, bsend, brecv, csend, crecv, gpbuf,
    q_s, q_r, do_s, do_r, kv_s, kv_r, p_s, p_r, o_s, o_r, dq_s, dq_r, dkv_s, dkv_r,
    a_s, a_r, b_s, b_r, c_s, c_r, g_s,
):
    dp = lax.axis_index("dp")
    me = lax.axis_index("head")
    x, yh = me // 2, lax.rem(me, 2)
    z, yl, core = dp // 4, lax.rem(dp // 2, 2), lax.rem(dp, 2)

    def slot_of(zz, yy, cc):
        return (lax.rem(zz + 4, 4) * 2 + yy) * 2 + cc

    other_core = (slot_of(z, yl, 1 - core), me)
    other_y = (slot_of(z, 1 - yl, core), me)
    up = (slot_of(z + 1, yl, core), me)
    down = (slot_of(z - 1, yl, core), me)
    steps = [(2, 1), (1, 0), (3, 1), (2, 0), (1, 1), (3, 0), (0, 1)]
    peers = [lax.rem(x + a, 4) * 2 + lax.rem(yh + b, 2) for a, b in steps]

    barrier = pltpu.get_barrier_semaphore()
    friends = [(dp, h) for h in peers] + [other_core, other_y, up, down]
    for friend in friends:
        pl.semaphore_signal(barrier, inc=1, device_id=friend, device_id_type=MESH)
    pl.semaphore_wait(barrier, len(friends))

    def send(src, dst, ssem, rsem, to):
        pltpu.make_async_remote_copy(
            src_ref=src, dst_ref=dst, send_sem=ssem, recv_sem=rsem, device_id=to, device_id_type=MESH
        ).start()

    def local(src, dst, sem):
        pltpu.make_async_copy(src, dst, sem).start()

    def drain(ref, sem):
        pltpu.make_async_copy(ref, ref, sem).wait()

    def mix(*queues):
        for turn in range(max(len(queue) for queue in queues)):
            for queue in queues:
                if turn < len(queue):
                    queue[turn]()

    def pieces(src, dst, ssem, rsem, to):
        rows = src.shape[0] // SPLIT
        return [
            functools.partial(
                send, src.at[pl.ds(n * rows, rows)], dst.at[pl.ds(n * rows, rows)], ssem, rsem, to
            )
            for n in range(SPLIT)
        ]

    mine = slot_of(z, yl, core)
    own_half = [
        pieces(pk_hbm, pbuf.at[mine], p_s, p_r.at[mine], to) for to in (other_y, up, down)
    ]
    send(pk_hbm, pbuf.at[mine], p_s, p_r.at[mine], other_core)
    local(pk_hbm, pbuf.at[mine], p_r.at[mine])

    def cols(h, width, offset=0):
        return pl.ds(pl.multiple_of(h * (width) + offset, DH), width)

    mix(
        *own_half,
        [
            functools.partial(
                send, kv_hbm.at[:, cols(h, WIDE)], kvbuf.at[me], kv_s, kv_r, (dp, h)
            )
            for h in peers
        ],
    )
    local(kv_hbm.at[:, cols(me, WIDE)], kvbuf.at[me], kv_r)

    def heads_of(h, c):
        return pl.ds(pl.multiple_of(h * SPAN + c * CW, DH), CW)

    def push_one(src, buf, ssem, rsem, c):
        local(src.at[:, heads_of(me, c)], buf.at[c, me], rsem.at[c])
        return [
            functools.partial(
                send, src.at[:, heads_of(h, c)], buf.at[c, me], ssem, rsem.at[c], (dp, h)
            )
            for h in peers
        ]

    def push_q(c):
        return push_one(q_hbm, qbuf, q_s, q_r, c)

    def push_do(c):
        return push_one(do_hbm, dobuf, do_s, do_r, c)

    def push(c, carry):
        mix(push_q(c), push_do(c))
        return carry

    def arrived(slot):
        drain(pbuf.at[slot], p_r.at[slot])
        send(pbuf.at[slot], pbuf.at[slot], p_s, p_r.at[slot], other_core)

    def onward(slot, to):
        return pieces(pbuf.at[slot], pbuf.at[slot], p_s, p_r.at[slot], to)

    near = slot_of(z, 1 - yl, core)
    arrived(near)
    mix(onward(near, up), onward(near, down), push_q(0), push_do(0))
    arrived(slot_of(z + 1, 0, core))
    arrived(slot_of(z - 1, 1, core))
    mix(
        push_q(1),
        onward(slot_of(z + 1, 0, core), down),
        onward(slot_of(z - 1, 1, core), up),
    )
    arrived(slot_of(z + 1, 1, core))
    arrived(slot_of(z - 1, 0, core))
    mix(push_do(1))
    dkbuf[...] = jnp.zeros_like(dkbuf)
    dvbuf[...] = jnp.zeros_like(dvbuf)
    drain(kvbuf, kv_r)
    for r in range(2):
        for b in range(4):
            rows = slice(PL + b * BLK, PL + (b + 1) * BLK)
            both = kvbuf[r * 4 + b]
            kbuf[r, rows] = both[:, :DH]
            vbuf[r, rows] = both[:, DH:]
            ktbuf[r, :, rows] = both[:, :DH].T
            vtbuf[r, :DH, rows] = both[:, DH:].T
        vtbuf[r, DH:] = jnp.ones((16, KEYS), BF)
    arrived(slot_of(z + 2, 0, core))
    arrived(slot_of(z + 2, 1, core))
    lax.fori_loop(2, CH, push, 0)
    drain(pbuf.at[mine], p_r.at[mine])
    for zz in range(4):
        for yy in range(2):
            slot = slot_of(zz, yy, 1 - core)
            drain(pbuf.at[slot], p_r.at[slot])

    need = [[po[2 * rp[r] + half] for half in range(2)] for r in range(2)]
    for r in range(2):
        for half in range(2):
            rows = slice(half * PLH, (half + 1) * PLH)
            both = pbuf[need[r][half]]
            kbuf[r, rows] = both[:, :DH]
            vbuf[r, rows] = both[:, DH:]
            ktbuf[r, :, rows] = both[:, :DH].T
            vtbuf[r, :DH, rows] = both[:, DH:].T

    def give(c):
        queues = []
        for buf, hbm, ssem, rsem in ((obuf, o_hbm, o_s, o_r), (dqbuf, dq_hbm, dq_s, dq_r)):
            local(buf.at[c, me], hbm.at[:, heads_of(me, c)], rsem)
            queues.append(
                [
                    functools.partial(
                        send, buf.at[c, h], hbm.at[:, heads_of(me, c)], ssem, rsem, (dp, h)
                    )
                    for h in peers
                ]
            )
        return queues

    def work(i, carry):
        c, r = i // 2, lax.rem(i, 2)

        @pl.when(r == 0)
        def _():
            drain(qbuf.at[c], q_r.at[c])
            drain(dobuf.at[c], do_r.at[c])

        for first in range(0, 4, NB):
            tiles = [(r * 4 + first + b, j) for b in range(NB) for j in range(GH)]
            q = jnp.concatenate([qbuf[c, h, :, j * DH : (j + 1) * DH] for h, j in tiles], axis=0)
            do = jnp.concatenate([dobuf[c, h, :, j * DH : (j + 1) * DH] for h, j in tiles], axis=0)
            w = first // NB % 2
            out, dq = attend(
                first, q, do, kbuf.at[r], vbuf.at[r], ktbuf.at[r], vtbuf.at[r],
                sbuf.at[w], ebuf.at[w], dbuf.at[w], dkbuf.at[r], dvbuf.at[r],
            )
            for i_, (h, j) in enumerate(tiles):
                obuf[c, h, :, j * DH : (j + 1) * DH] = out[i_ * BLK : (i_ + 1) * BLK]
                dqbuf[c, h, :, j * DH : (j + 1) * DH] = dq[i_ * BLK : (i_ + 1) * BLK]

        @pl.when((r == 1) & (c < CH - HELD))
        def _():
            mix(*give(c))

        return carry

    lax.fori_loop(0, CH * 2, work, 0)

    def partial(slot):
        total = None
        for r in range(2):
            for half in range(2):
                rows = slice(half * PLH, (half + 1) * PLH)
                pick = jnp.where(need[r][half] == slot, 1.0, 0.0).astype(F32)
                block = jnp.concatenate(
                    [dkbuf[r, rows] * (pick * SCALE), dvbuf[r, rows] * pick], axis=1
                )
                total = block if total is None else total + block
        return total

    def pair_of(hop, yy):
        return lax.rem(z + hop, 4) * 2 + yy

    order = [(2, 0), (2, 1), (1, 1), (3, 0), (1, 0), (3, 1), (0, 0), (0, 1)]
    for hop, yy in order:
        n = pair_of(hop, yy)
        asend[n] = partial(n * 2 + (1 - core)).astype(BF)
        send(asend.at[n], arecv.at[n], a_s, a_r.at[n], other_core)

    def own_pair(hop, yy):
        n = pair_of(hop, yy)
        total = partial(n * 2 + core)
        drain(arecv.at[n], a_r.at[n])
        return total + arecv[n].astype(F32)

    def along(i, value, to):
        bsend[i] = value.astype(BF)
        return pieces(bsend.at[i], brecv.at[i], b_s, b_r.at[i], to)

    first_up = along(0, own_pair(2, 0), up)
    first_down = along(1, own_pair(2, 1), down)
    mix(first_up, first_down)
    second_up = along(2, own_pair(1, 1), up)
    second_down = along(3, own_pair(3, 0), down)
    mix(second_up, second_down)
    last = []
    for i, hop, yy, to in ((0, 1, 0, up), (1, 3, 1, down)):
        total = own_pair(hop, yy)
        drain(brecv.at[i], b_r.at[i])
        last.append(along(4 + i, total + brecv[i].astype(F32), to))

    for b in range(8):
        r, at = b // 4, PL + (b % 4) * BLK
        dkvbuf[b, :, :DH] = (dkbuf[r, at : at + BLK] * SCALE).astype(BF)
        dkvbuf[b, :, DH:] = dvbuf[r, at : at + BLK].astype(BF)
    pairs_out = [
        functools.partial(
            send, dkvbuf.at[h], dkv_hbm.at[:, cols(me, WIDE)], dkv_s, dkv_r, (dp, h)
        )
        for h in peers
    ]
    local(dkvbuf.at[me], dkv_hbm.at[:, cols(me, WIDE)], dkv_r)
    mix(*last, pairs_out, *give(CH - 1))

    zero_half = own_pair(0, 0)
    one_half = own_pair(0, 1)
    for i in (2, 3, 4, 5):
        drain(brecv.at[i], b_r.at[i])
    zero_half += brecv[3].astype(F32) + brecv[4].astype(F32)
    one_half += brecv[2].astype(F32) + brecv[5].astype(F32)
    low = yl == 0
    csend[...] = jnp.where(low, one_half, zero_half).astype(BF)
    mix(pieces(csend, crecv, c_s, c_r, other_y))
    kept = jnp.where(low, zero_half, one_half)
    drain(crecv, c_r)
    gpbuf[...] = (kept + crecv[...].astype(F32)).astype(BF)
    local(gpbuf, gp_hbm, g_s)

    drain(gp_hbm, g_s)
    drain(o_hbm, o_r)
    drain(dq_hbm, dq_r)
    drain(dkv_hbm, dkv_r)
    drain(q_hbm.at[:, : 7 * SPAN], q_s)
    drain(do_hbm.at[:, : 7 * SPAN], do_s)
    drain(kv_hbm.at[:, : 7 * WIDE], kv_s)
    drain(pbuf.at[0:15], p_s)
    drain(obuf.at[:, 0:7], o_s)
    drain(dqbuf.at[:, 0:7], dq_s)
    drain(dkvbuf.at[0:7], dkv_s)
    drain(asend, a_s)
    drain(bsend, b_s)
    drain(csend, c_s)


def settle(*refs):
    sources, targets, stages = refs[:4], refs[4:8], refs[8:12]
    into, out = refs[12:]
    moves = []
    for src, dst, stage, parts in zip(sources, targets, stages, PARTS):
        rows = src.shape[0] // parts
        for n in range(parts):
            at, i = pl.ds(n * rows, rows), len(moves)
            moves.append(
                (
                    pltpu.make_async_copy(src.at[at], stage.at[at], into.at[i]),
                    pltpu.make_async_copy(stage.at[at], dst.at[at], out.at[i]),
                )
            )
    for first, _ in moves:
        first.start()
    for first, second in moves:
        first.wait()
        second.start()
    for _, second in moves:
        second.wait()


def body(resp_query, resp_keyval, grad_out, prompt_keyval, response_prompt, piece_owner):
    tok = resp_query.shape[0]
    hbm = pl.BlockSpec(memory_space=pl.ANY)
    smem = pl.BlockSpec(memory_space=pltpu.SMEM)
    dma = pltpu.SemaphoreType.DMA
    shapes = [
        pltpu.VMEM((CH, 8, BLK, CW), BF),
        pltpu.VMEM((CH, 8, BLK, CW), BF),
        pltpu.VMEM((8, BLK, WIDE), BF),
        pltpu.VMEM((16, PLH, WIDE), BF),
        pltpu.VMEM((2, KEYS, DH), BF),
        pltpu.VMEM((2, KEYS, DH), BF),
        pltpu.VMEM((2, DH, KEYS), BF),
        pltpu.VMEM((2, DH + 16, KEYS), BF),
        pltpu.VMEM((2, KEYS, ROWS), F32),
        pltpu.VMEM((2, KEYS, ROWS), BF),
        pltpu.VMEM((2, KEYS, ROWS), BF),
        pltpu.VMEM((2, KEYS, DH), F32),
        pltpu.VMEM((2, KEYS, DH), F32),
        pltpu.VMEM((CH, 8, BLK, CW), BF),
        pltpu.VMEM((CH, 8, BLK, CW), BF),
        pltpu.VMEM((8, BLK, WIDE), BF),
        pltpu.VMEM((8, PLH, WIDE), BF),
        pltpu.VMEM((8, PLH, WIDE), BF),
        pltpu.VMEM((6, PLH, WIDE), BF),
        pltpu.VMEM((6, PLH, WIDE), BF),
        pltpu.VMEM((PLH, WIDE), BF),
        pltpu.VMEM((PLH, WIDE), BF),
        pltpu.VMEM((PLH, WIDE), BF),
    ]
    sems = [
        dma, dma((CH,)), dma, dma((CH,)), dma, dma, dma, dma((16,)),
        dma, dma, dma, dma, dma, dma,
        dma, dma((8,)), dma, dma((6,)), dma, dma, dma,
    ]
    made = pl.pallas_call(
        kernel,
        out_shape=[
            jax.ShapeDtypeStruct((tok, 8 * SPAN), BF),
            jax.ShapeDtypeStruct((tok, 8 * SPAN), BF),
            jax.ShapeDtypeStruct((tok, 8 * WIDE), BF),
            jax.ShapeDtypeStruct((PLH, WIDE), BF),
        ],
        in_specs=[hbm, hbm, hbm, hbm, smem, smem],
        out_specs=[hbm, hbm, hbm, hbm],
        scratch_shapes=shapes + sems,
        compiler_params=pltpu.CompilerParams(
            collective_id=0, has_side_effects=True, vmem_limit_bytes=60 * 2**20
        ),
        name="attention",
    )(resp_query, grad_out, resp_keyval, prompt_keyval, response_prompt, piece_owner)
    return pl.pallas_call(
        settle,
        out_shape=[jax.ShapeDtypeStruct(a.shape, a.dtype) for a in made],
        in_specs=[hbm] * 4,
        out_specs=[hbm] * 4,
        scratch_shapes=[pltpu.VMEM(a.shape, a.dtype) for a in made] + [dma((sum(PARTS),))] * 2,
        compiler_params=pltpu.CompilerParams(vmem_limit_bytes=60 * 2**20),
        name="settle",
    )(*made)


def solution(mesh):
    rows = P(("dp", "head"), None)
    placed = (rows, rows, rows, P("dp", "head"), P("dp"), P())
    return jax.shard_map(
        body,
        mesh=mesh,
        in_specs=placed,
        out_specs=(rows, rows, rows, P("dp", "head")),
        check_vma=False,
    )
```
